512 devices in a mesh: corpus: 64 (over x, z), mp: 8 (over y, core).
Axes of the slice: x: 4, y: 4, z: 16, core: 2. Of those that a mesh axis runs over, the one named last changes fastest.
Arguments:
- question_word_vectors: bfloat16 [16, 32, 128], P('mp'), may hold values from -0.29882812 to 0.29882812
- document_word_vectors: bfloat16 [4096, 128, 128], P('corpus'), may hold values from -0.5 to 0.5
- document_extent: int32 [4096], P('corpus'), may hold values from 4 to 128
- shortlist_documents: int32 [16, 1024], P('mp'), may hold values from 0 to 4095, all different within a row
- retained_documents: int32 [16, 2], replicated, may hold values from 0 to 4095
- document_vocab_codes: int32 [4096, 32], P('corpus'), may hold values from 0 to 76799
- vocab_lookup_table: bfloat16 [76800, 4096], P('corpus', 'mp')
- prelayer_rms_gain: bfloat16 [4096], P('mp'), may hold values from 0.099609375 to 1.8984375
- gating_projector: bfloat16 [4096, 12288], P('mp', 'corpus'), may hold values from -0.09375 to 0.09375
- widening_projector: bfloat16 [4096, 12288], P('mp', 'corpus'), may hold values from -0.09375 to 0.09375
- reducing_projector: bfloat16 [12288, 4096], P('corpus', 'mp'), may hold values from -0.0546875 to 0.0546875
- merit_readout: float32 [4096], P('mp'), may hold values from -0.5 to 0.5
Outputs:
- shortlist_maxsim: float32 [16, 1024], replicated
- layer_result: bfloat16 [1024, 4096], P('corpus', 'mp')
- retained_merit: float32 [16, 2], replicated
The draws below stay inside these ranges and needn't reach their ends.
Inputs may be any that keep to these rules, and one draw needn't show every extreme that they name: `shortlist_documents`: each row of candidates names 1024 different passages.
All inputs are finite; a program needn't handle non-finite values.
Results may differ from the reference program's by a relative error of at most 0.0034.
Values may be sent and summed in bfloat16 or wider, within the bound.
No kernel may reach another device: no remote copies, remote signals or barrier semaphores. Data moves between devices by JAX's collectives and lax.ppermute only.
A program may use at most 64 MiB of HBM per device.

```python
import math
import jax
import jax.numpy as jnp
import numpy as np
from jax import lax

D = 4096
FF = 12288
CDIM = 128
QTOK = 32
PLEN = 128
PASS_DEV = 64
QUESTION_NUMBER = 16
CAND = 1024
KEPT_PER_ASKING = 2
POSITION_SPAN = 32
VOCAB = 76800
DOCUMENT_NUMBER = 4096
KEPT_OVERALL = 32
TOKENS = 1024
N_CORPUS = 64


def draw_vocab_lookup_table(key, part):
    key = jax.random.fold_in(key, 7)
    key_values, key_rows = jax.random.split(key)
    column_scale = 10.0 ** (jnp.arange(D, dtype=jnp.float32) / D)
    row_scale = 10.0 ** jax.random.uniform(key_rows, (VOCAB, 1), jnp.float32)
    values = jax.random.normal(key_values, (VOCAB, D), jnp.float32)
    return (0.1 * values * column_scale[None, :] * row_scale).astype(jnp.bfloat16)


def plant(array, own_key, low, largest):
    longest = array.shape.index(max(array.shape))
    spots = []
    for shift in (0, 1):
        where = [jax.random.randint(jax.random.fold_in(own_key, axis), (), 0, length) for axis, length in enumerate(array.shape)]
        where[longest] = (where[longest] + shift) % array.shape[longest]
        spots.append(tuple(where))
    return array.at[spots[0]].set(low).at[spots[1]].set(largest)


def block_scale(own_key, extent, cuts, smallest, top_value):
    def one(position, shards_of):
        draws = jax.random.uniform(jax.random.fold_in(jax.random.fold_in(own_key, 6), position), (shards_of,), jnp.float32, smallest / len(cuts), top_value / len(cuts))
        return jnp.repeat(jnp.exp(draws), extent[position] // shards_of).reshape((-1,) + (1,) * (len(extent) - position - 1))

    factor_of = one(*cuts[0])
    for cut in cuts[1:]:
        factor_of = factor_of * one(*cut)
    return factor_of


def wide_ids(stream_key, shape, count, lean):
    portions = [min(1 << octave, count + 1 - (1 << octave)) * (1 << 20) // math.isqrt((1 << octave) ** lean) + 1 for octave in range((count + 1).bit_length()) if 1 << octave <= count]
    spread = 1 + sum(portions) // (1 << 30)
    grid = np.cumsum(np.array([max(1, weight // spread) for weight in portions]))
    ticket = jax.random.randint(jax.random.fold_in(stream_key, 1), shape, 0, int(grid[len(portions) - 1]))
    start = jnp.left_shift(1, jnp.searchsorted(jnp.asarray(grid, jnp.int32), ticket, side="right").astype(jnp.int32))
    rank = start - 1 + jax.random.randint(jax.random.fold_in(stream_key, 4), shape, 0, 1 << 30) % jnp.minimum(start, count + 1 - start)
    return jax.random.permutation(jax.random.fold_in(stream_key, 2), count)[rank].astype(jnp.int32)


def distinct(own_key, rows, count, top, lift):
    sequence = jax.random.permutation(jax.random.fold_in(own_key, 1), count)
    pull = sequence
    for power in range(3):
        pull = pull * pull // count
    pull = pull * lift // count
    chance = jax.random.randint(jax.random.fold_in(own_key, 2), (rows, count), 0, 4096) + pull
    sure = jax.random.permutation(jax.random.fold_in(own_key, 3), rows)[jnp.arange(count) % rows]
    chance = jnp.where(jnp.arange(rows)[:, None] == sure[None, :], 1 << 14, chance)
    merit = chance * count + jnp.arange(count)
    return lax.top_k(merit.astype(jnp.int32), top)[1].astype(jnp.int32)


def gaussian(stream_key, extent, width, most, cuts=(), held_as=jnp.bfloat16):
    entries = jax.random.normal(stream_key, extent, jnp.float32) * width
    if len(cuts) > 0:
        entries = block_scale(stream_key, extent, cuts, -0.22, 0.18) * entries
    return jnp.clip(entries, min=-most, max=most).astype(held_as)


def setup_inputs(seed: int = 0) -> dict:
    key_of = jax.random.split(jax.random.key(seed), 13)
    return {
        "question_word_vectors": gaussian(key_of[0], (QUESTION_NUMBER, QTOK, CDIM), 0.05, 0.29882812, ((0, 8),)),
        "document_word_vectors": gaussian(key_of[1], (DOCUMENT_NUMBER, PLEN, CDIM), CDIM ** -0.5, 0.5, ((0, 64),)),
        "document_extent": plant(jax.random.randint(key_of[2], (DOCUMENT_NUMBER,), 4, PLEN + 1), jax.random.fold_in(key_of[2], 1), 4, PLEN).astype(jnp.int32),
        "shortlist_documents": distinct(key_of[3], QUESTION_NUMBER, DOCUMENT_NUMBER, CAND, 4096),
        "retained_documents": plant(jax.random.randint(key_of[4], (QUESTION_NUMBER, KEPT_PER_ASKING), 0, DOCUMENT_NUMBER), jax.random.fold_in(key_of[4], 1), 0, DOCUMENT_NUMBER - 1).astype(jnp.int32),
        "document_vocab_codes": plant(wide_ids(key_of[5], (DOCUMENT_NUMBER, POSITION_SPAN), VOCAB, 2), jax.random.fold_in(key_of[5], 3), 0, VOCAB - 1).astype(jnp.int32),
        "vocab_lookup_table": draw_vocab_lookup_table(jax.random.fold_in(key_of[12], 71), 0),
        "prelayer_rms_gain": jnp.clip(1.0 + 0.18 * jax.random.normal(key_of[7], (D,), jnp.float32), 0.099609375, 1.8984375).astype(jnp.bfloat16),
        "gating_projector": gaussian(key_of[8], (D, FF), D ** -0.5, 0.09375, ((0, 8), (1, 64))),
        "widening_projector": gaussian(key_of[9], (D, FF), D ** -0.5, 0.09375, ((0, 8), (1, 64))),
        "reducing_projector": gaussian(key_of[10], (FF, D), FF ** -0.5, 0.0546875, ((0, 64), (1, 8))),
        "merit_readout": gaussian(key_of[11], (D,), 0.08, 0.5, ((0, 8),), jnp.float32),
    }


def reference(question_word_vectors, document_word_vectors, document_extent, shortlist_documents, retained_documents, document_vocab_codes, vocab_lookup_table, prelayer_rms_gain, gating_projector, widening_projector, reducing_projector, merit_readout):
    flat_queries = question_word_vectors.reshape(QUESTION_NUMBER * QTOK, CDIM)
    vector_blocks = document_word_vectors.reshape(N_CORPUS, PASS_DEV * PLEN, CDIM)
    length_blocks = document_extent.reshape(N_CORPUS, PASS_DEV)

    def block_scores(pair):
        vectors, lengths = pair
        dots = lax.dot_general(flat_queries, vectors, (((1,), (1,)), ((), ())), preferred_element_type=jnp.float32)
        dots = dots.reshape(QUESTION_NUMBER, QTOK, PASS_DEV, PLEN)
        valid = jnp.arange(PLEN, dtype=jnp.int32)[None, :] < lengths[:, None]
        best = lax.optimization_barrier(jnp.max(jnp.where(valid[None, None], dots, jnp.float32(-1e+30)), axis=3))
        return lax.optimization_barrier(jnp.sum(best, axis=1))
    per_block = lax.map(block_scores, (vector_blocks, length_blocks))
    passage_scores = jnp.transpose(per_block, (1, 0, 2)).reshape(QUESTION_NUMBER, DOCUMENT_NUMBER)
    shortlist_maxsim = jnp.take_along_axis(passage_scores, shortlist_documents, axis=1)
    chosen_positions = retained_documents.reshape(KEPT_OVERALL)
    texts = document_vocab_codes[chosen_positions]
    seq_len = jnp.minimum(document_extent[chosen_positions], POSITION_SPAN)
    token_ids = texts.reshape(TOKENS)
    embedded = vocab_lookup_table[token_ids]
    wide = embedded.astype(jnp.float32)
    mean_square = lax.optimization_barrier(jnp.mean(wide * wide, axis=1))
    rscale = lax.rsqrt(mean_square + 1e-06)
    scaled = (wide * prelayer_rms_gain.astype(jnp.float32)).astype(jnp.bfloat16)
    gate = rscale[:, None] * jnp.dot(scaled, gating_projector, preferred_element_type=jnp.float32)
    up_proj = rscale[:, None] * jnp.dot(scaled, widening_projector, preferred_element_type=jnp.float32)
    hidden = (jax.nn.silu(gate) * up_proj).astype(jnp.bfloat16)
    total = wide + jnp.dot(hidden, reducing_projector, preferred_element_type=jnp.float32)
    layer_result = total.astype(jnp.bfloat16)
    per_token = lax.optimization_barrier(jnp.sum(total * merit_readout[None, :], axis=1))
    slot_index = jnp.arange(TOKENS, dtype=jnp.int32)
    seq_of_row = slot_index // POSITION_SPAN
    row_len = seq_len[seq_of_row]
    readout_product = jnp.where(slot_index % POSITION_SPAN < row_len, per_token, jnp.float32(0.0)) / row_len.astype(jnp.float32)
    retained_merit = lax.optimization_barrier(jnp.sum(readout_product.reshape(KEPT_OVERALL, POSITION_SPAN), axis=1)).reshape(QUESTION_NUMBER, KEPT_PER_ASKING)
    return (shortlist_maxsim, layer_result, retained_merit)
```

```python
import jax
import jax.numpy as jnp
from jax import lax
from jax.sharding import Mesh, PartitionSpec as P

NX, NZ = 4, 16
F32, BF16 = jnp.float32, jnp.bfloat16


def split3(v):
    high = lax.reduce_precision(v, 8, 7)
    rest = v - high
    mid = lax.reduce_precision(rest, 8, 7)
    low = lax.reduce_precision(rest - mid, 8, 7)
    return jnp.stack([high, mid, low]).astype(BF16)


def join3(parts, axis=0):
    return jnp.sum(parts.astype(F32), axis=axis)


def swap(v, axis):
    return lax.all_to_all(v, axis, 0, 0, tiled=True)


def share(v, axis, n):
    return swap(jnp.broadcast_to(v[None], (n, *v.shape)), axis)


def rows_of(values, rows, columns):
    flat = values.reshape(-1)
    return jnp.pad(flat, (0, rows * columns - flat.shape[0])).reshape(rows, columns)


def body(
    question_word_vectors,
    document_word_vectors,
    document_extent,
    shortlist_documents,
    retained_documents,
    document_vocab_codes,
    vocab_lookup_table,
    prelayer_rms_gain,
    gating_projector,
    widening_projector,
    reducing_projector,
    merit_readout,
):
    n_mp = lax.axis_size("mp")
    corpus_index = lax.axis_index("x") * NZ + lax.axis_index("z")
    query_count = question_word_vectors.shape[0]
    pass_count, pass_slots, vector_dim = document_word_vectors.shape
    width = vocab_lookup_table.shape[1]
    hidden_units = gating_projector.shape[1]
    seq_count = retained_documents.size
    seq_width = document_vocab_codes.shape[1]
    tokens = seq_count * seq_width

    with jax.named_scope("token_ids"):
        pass_offset = corpus_index * pass_count
        chosen = retained_documents.reshape(-1) - pass_offset
        mine = chosen[:, None] == jnp.arange(pass_count, dtype=jnp.int32)[None, :]
        valid = jnp.arange(seq_width, dtype=jnp.int32)[None, :] < document_extent[:, None]
        coded = document_vocab_codes * 2 + valid.astype(jnp.int32)
        coded = jnp.sum(jnp.where(mine[:, :, None], coded[None], 0), axis=1)
        coded = coded.reshape(tokens // 128, 128)
        coded = jnp.sum(share(coded, "z", NZ), axis=0)
        coded = jnp.sum(share(coded, "x", NX), axis=0)
        coded = coded.reshape(tokens)
        token_ids = coded // 2
        token_valid = (coded % 2).reshape(seq_count, seq_width)
        weight = token_valid.astype(F32) / jnp.sum(token_valid, axis=1, keepdims=True).astype(F32)

    with jax.named_scope("passage_scores"):
        dots = lax.dot_general(
            question_word_vectors.reshape(-1, vector_dim),
            document_word_vectors.reshape(-1, vector_dim),
            (((1,), (1,)), ((), ())),
            preferred_element_type=F32,
        ).reshape(query_count, -1, pass_count, pass_slots)
        slots = jnp.arange(pass_slots, dtype=jnp.int32)[None, :] < document_extent[:, None]
        best = jnp.max(jnp.where(slots[None, None], dots, F32(-1e30)), axis=3)
        scores = jnp.sum(best, axis=1)

    with jax.named_scope("embedded"):
        vocab_rows = vocab_lookup_table.shape[0]
        local_ids = token_ids - corpus_index * vocab_rows
        chosen_rows = (
            local_ids[:, None] == jnp.arange(vocab_rows, dtype=jnp.int32)[None, :]
        ).astype(BF16)
        looked = jnp.dot(chosen_rows, vocab_lookup_table, preferred_element_type=F32).astype(BF16)
        looked = swap(looked.reshape(NX, tokens // NX, width), "x")
        looked = jnp.sum(looked.astype(F32), axis=0).astype(BF16)
        looked = swap(looked.reshape(NZ, -1, width), "z")
        own_rows = jnp.sum(looked.astype(F32), axis=0)
        share_rows = own_rows.shape[0]
        score_rows = rows_of(split3(scores), 8, width)
        block = jnp.concatenate([own_rows.astype(BF16), score_rows], axis=0)
        block = share(block, "z", NZ).reshape(-1, width)
        block = share(block, "x", NX).reshape(NX * NZ, share_rows + 8, width)
        embedded = block[:, :share_rows].reshape(tokens, width)
        all_scores = block[:, share_rows:].reshape(NX * NZ, -1)[:, : 3 * scores.size]
        all_scores = join3(all_scores.reshape(NX * NZ, 3, query_count, pass_count), axis=1)
        all_scores = jnp.transpose(all_scores, (1, 0, 2)).reshape(query_count, -1)

    with jax.named_scope("shortlist"):
        high, low = shortlist_documents // 128, shortlist_documents % 128
        at_high = (high[:, :, None] == jnp.arange(all_scores.shape[1] // 128)[None, None]).astype(F32)
        table = all_scores.reshape(query_count, -1, 128)
        lines = lax.dot_general(
            at_high, table, (((2,), (1,)), ((0,), (0,))), precision=lax.Precision.HIGHEST
        )
        at_low = low[:, :, None] == jnp.arange(128)[None, None]
        picked = jnp.sum(jnp.where(at_low, lines, F32(0.0)), axis=2)

    with jax.named_scope("gate_up"):
        wide = embedded.astype(F32)
        squares = jnp.sum(wide * wide, axis=1)
        readings = jnp.sum(wide * merit_readout[None, :], axis=1)
        scaled = (wide * prelayer_rms_gain.astype(F32)).astype(BF16)
        both = jnp.concatenate([gating_projector, widening_projector], axis=1)
        part = jnp.dot(scaled, both, preferred_element_type=F32).astype(BF16)
        part = part.reshape(n_mp, tokens // n_mp, 2 * hidden_units)
        sums = jnp.stack([squares.reshape(n_mp, -1), readings.reshape(n_mp, -1)], axis=1)
        sums = jnp.moveaxis(split3(sums), 0, 1).reshape(n_mp, -1)
        sums = jnp.pad(sums, ((0, 0), (0, 16 * hidden_units - sums.shape[1])))
        part = jnp.concatenate([part, sums.reshape(n_mp, 8, 2 * hidden_units)], axis=1)
        part = swap(part, "mp")
        total_part = jnp.sum(part[:, : tokens // n_mp].astype(F32), axis=0)
        sums = part[:, tokens // n_mp :].reshape(n_mp, -1)[:, : 6 * (tokens // n_mp)]
        sums = jnp.sum(sums.astype(F32).reshape(n_mp * 3, 2, tokens // n_mp), axis=0)
        rscale = lax.rsqrt(sums[0] / (n_mp * width) + 1e-06)[:, None]
        gate, up = total_part[:, :hidden_units], total_part[:, hidden_units:]
        hidden = (jax.nn.silu(rscale * gate) * (rscale * up)).astype(BF16)

    with jax.named_scope("hidden"):
        extra = jnp.concatenate([split3(sums[1]).reshape(-1), split3(picked).reshape(-1)])
        extra_rows = -(-extra.size // (hidden_units * 16)) * 16
        block = jnp.concatenate([hidden, rows_of(extra, extra_rows, hidden_units)], axis=0)
        block = share(block, "mp", n_mp)
        hidden = block[:, : tokens // n_mp].reshape(tokens, hidden_units)
        extra = block[:, tokens // n_mp :].reshape(n_mp, -1)
        cut = 3 * tokens // n_mp
        readings = join3(extra[:, :cut].reshape(n_mp, 3, -1), axis=1).reshape(tokens)
        shortlist_maxsim = join3(
            extra[:, cut : cut + 3 * picked.size].reshape(n_mp, 3, *picked.shape), axis=1
        ).reshape(-1, picked.shape[1])

    with jax.named_scope("down"):
        line = lax.psum(
            jnp.sum(reducing_projector.astype(F32) * merit_readout[None, :], axis=1), "mp"
        )
        merit = jnp.sum(hidden.astype(F32) * line[None, :], axis=1)
        merit = jnp.sum(merit.reshape(seq_count, seq_width) * weight, axis=1)
        down = jnp.dot(hidden, reducing_projector, preferred_element_type=F32).astype(BF16)
        down = down.reshape(NX, tokens // NX, width)
        rider = rows_of(split3(merit), 8, width)
        down = jnp.concatenate([down, jnp.broadcast_to(rider[None], (NX, 8, width))], axis=1)
        down = swap(down, "x")
        rider = down[:, tokens // NX :].reshape(NX, -1)[:, : 3 * seq_count]
        merit = jnp.sum(rider.reshape(NX * 3, seq_count).astype(F32), axis=0)
        down = jnp.sum(down[:, : tokens // NX].astype(F32), axis=0).astype(BF16)
        down = down.reshape(NZ, -1, width)
        rider = rows_of(split3(merit), 8, width)
        down = jnp.concatenate([down, jnp.broadcast_to(rider[None], (NZ, 8, width))], axis=1)
        down = swap(down, "z")
        rider = down[:, share_rows:].reshape(NZ, -1)[:, : 3 * seq_count]
        merit = jnp.sum(rider.reshape(NZ * 3, seq_count).astype(F32), axis=0)
        total = own_rows + jnp.sum(down[:, :share_rows].astype(F32), axis=0)
        layer_result = total.astype(BF16)
        merit = merit + jnp.sum(readings.reshape(seq_count, seq_width) * weight, axis=1)

    return (shortlist_maxsim, layer_result, merit.reshape(retained_documents.shape))


def solution(mesh):
    split = Mesh(mesh.devices.reshape(NX, NZ, -1), ("x", "z", "mp"))
    corpus = ("x", "z")
    placed = (
        P("mp", None, None),
        P(corpus, None, None),
        P(corpus),
        P("mp", None),
        P(),
        P(corpus, None),
        P(corpus, "mp"),
        P("mp"),
        P("mp", corpus),
        P("mp", corpus),
        P(corpus, "mp"),
        P("mp"),
    )
    return jax.shard_map(
        body, mesh=split, in_specs=placed, out_specs=(P(), P(corpus, "mp"), P()), check_vma=False
    )
```

```python
import functools

import jax
import jax.numpy as jnp
from jax import lax
from jax.experimental import pallas as pl
from jax.experimental.pallas import tpu as pltpu
from jax.sharding import Mesh, PartitionSpec as P

NX, NZ = 4, 16
LANES = 128
F32, BF16 = jnp.float32, jnp.bfloat16
CORPUS = ("x", "z")
TRANSPOSED = (((1,), (1,)), ((), ()))


def split3(v):
    high = lax.reduce_precision(v, 8, 7)
    rest = v - high
    mid = lax.reduce_precision(rest, 8, 7)
    low = lax.reduce_precision(rest - mid, 8, 7)
    return jnp.stack([high, mid, low]).astype(BF16)


def swap(v, axis):
    return lax.all_to_all(v, axis, 0, 0, tiled=True)


def share_with(v, axis, n):
    return swap(jnp.broadcast_to(v[None], (n, *v.shape)), axis)


def terms(v):
    high = v.astype(BF16).astype(F32)
    mid = (v - high).astype(BF16).astype(F32)
    return high, mid, v - high - mid


def fill(shape, axis, pieces):
    place = lax.broadcasted_iota(jnp.int32, shape, axis)
    block = jnp.zeros(shape, F32)
    for i, piece in enumerate(pieces):
        block = jnp.where(place == i, piece, block)
    return block


def gate_up_kernel(
    n_mp, units, rows_ref, gain_ref, readout_ref, w0_ref, w1_ref, w2_ref, w3_ref, out_ref, first, second
):
    parts = (w0_ref, w1_ref, w2_ref, w3_ref)
    half = NX * units
    for i, part in enumerate(parts):
        first[i * units : (i + 1) * units, :] = part[:units, :]
        first[half + i * units : half + (i + 1) * units, :] = part[units : 2 * units, :]
        second[i * units : (i + 1) * units, :] = part[2 * units :, :]
    value = rows_ref[...].astype(F32)
    squares = jnp.sum(value * value, axis=1, keepdims=True)
    reading = jnp.sum(value * readout_ref[...], axis=1, keepdims=True)
    scaled = (value * gain_ref[...]).astype(BF16)
    both = lax.dot_general(scaled, first[...], TRANSPOSED, preferred_element_type=F32)
    per_token = fill((value.shape[0], LANES), 1, (*terms(squares), *terms(reading)))

    readout = fill((16, value.shape[1]), 0, terms(readout_ref[...])).astype(BF16)
    line = lax.dot_general(readout, second[...], TRANSPOSED, preferred_element_type=F32)
    line = jnp.sum(line, axis=0, keepdims=True)
    pieces = [
        term[:, at : at + LANES] for term in terms(line) for at in range(0, half, LANES)
    ]
    share = value.shape[0] // n_mp
    line = fill((share, LANES), 0, pieces).astype(BF16)
    for target in range(n_mp):
        take = slice(target * share, (target + 1) * share)
        out_ref[target, :, : 2 * half] = both[take].astype(BF16)
        out_ref[target, :, 2 * half : 2 * half + LANES] = per_token[take].astype(BF16)
        out_ref[target, :, 2 * half + LANES :] = line


def hidden_kernel(n_mp, features, half, got_ref, weight_ref, picks_ref, out_ref):
    total = got_ref[0].astype(F32)
    for source in range(1, n_mp):
        total += got_ref[source].astype(F32)
    per_token = total[:, 2 * half : 2 * half + LANES]
    lane = lax.broadcasted_iota(jnp.int32, per_token.shape, 1)
    squares = jnp.sum(jnp.where(lane < 3, per_token, 0.0), axis=1, keepdims=True)
    reading = jnp.sum(jnp.where((lane >= 3) & (lane < 6), per_token, 0.0), axis=1, keepdims=True)
    rscale = lax.rsqrt(squares / features + 1e-06)
    gate, up = rscale * total[:, :half], rscale * total[:, half : 2 * half]
    hidden = (gate / (1.0 + jnp.exp(-gate)) * up).astype(BF16)
    line = total[:, 2 * half + LANES :]
    count = half // LANES
    merit = reading * (1.0 / NZ)
    for i in range(count):
        piece = line[i : i + 1] + line[count + i : count + i + 1] + line[2 * count + i : 2 * count + i + 1]
        merit += jnp.sum(
            hidden[:, i * LANES : (i + 1) * LANES].astype(F32) * piece, axis=1, keepdims=True
        )
    merit = jnp.sum(merit * weight_ref[:, :1], axis=0, keepdims=True)
    place = lax.broadcasted_iota(jnp.int32, per_token.shape, 0)
    rider = picks_ref[:, LANES:].astype(F32)
    for i, term in enumerate(terms(merit)):
        rider = jnp.where(place == 16 + i, term, rider)
    out_ref[:, :half] = hidden
    out_ref[:, half : half + LANES] = picks_ref[:, :LANES]
    out_ref[:, half + LANES :] = rider.astype(BF16)


def down_kernel(n_mp, units, half, got_ref, w0_ref, w1_ref, w2_ref, w3_ref, out_ref, second):
    for i, part in enumerate((w0_ref, w1_ref, w2_ref, w3_ref)):
        second[i * units : (i + 1) * units, :] = part[2 * units :, :]
    tokens = got_ref.shape[0] * got_ref.shape[1]
    hidden = got_ref[:, :, :half].reshape(tokens, half)
    down = jnp.dot(hidden, second[...], preferred_element_type=F32)
    groups = out_ref.shape[0]
    share = tokens // groups
    shares = got_ref[:, 16:, half + LANES :].astype(F32)
    rider = fill((n_mp, LANES), 1, (shares[:, 0], shares[:, 1], shares[:, 2]))
    rider = jnp.concatenate([rider, jnp.zeros((share - n_mp, LANES), F32)], axis=0).astype(BF16)
    for target in range(groups):
        out_ref[target, :, : down.shape[1]] = down[target * share : (target + 1) * share].astype(BF16)
        out_ref[target, :, down.shape[1] :] = rider


def body(
    question_word_vectors,
    document_word_vectors,
    document_extent,
    shortlist_documents,
    retained_documents,
    document_vocab_codes,
    vocab_lookup_table,
    prelayer_rms_gain,
    gating_projector,
    widening_projector,
    reducing_projector,
    merit_readout,
):
    n_mp = lax.axis_size("mp")
    x_index, z_index, mp_index = (lax.axis_index(name) for name in ("x", "z", "mp"))
    corpus_index = x_index * NZ + z_index
    query_count = question_word_vectors.shape[0]
    pass_count, pass_slots, vector_dim = document_word_vectors.shape
    vocab_rows, width = vocab_lookup_table.shape
    units = gating_projector.shape[1]
    half = NX * units
    seq_count = retained_documents.size
    seq_width = document_vocab_codes.shape[1]
    tokens = seq_count * seq_width
    share = tokens // (NX * NZ)
    own_tokens = tokens // NX // n_mp

    with jax.named_scope("weights"):
        weights = [jnp.concatenate([gating_projector.T, widening_projector.T, reducing_projector], axis=0)]
        pairs = [(i, (i + 1) % NX) for i in range(NX)]
        for _ in range(1, NX):
            weights.append(lax.ppermute(weights[-1], "x", pairs))
        gain = prelayer_rms_gain.astype(F32)[None]
        readout = merit_readout[None]

    with jax.named_scope("token_ids"):
        chosen = retained_documents.reshape(-1) - corpus_index * pass_count
        mine = chosen[:, None] == jnp.arange(pass_count, dtype=jnp.int32)[None, :]
        valid = jnp.arange(seq_width, dtype=jnp.int32)[None, :] < document_extent[:, None]
        coded = document_vocab_codes * 2 + valid.astype(jnp.int32)
        coded = jnp.sum(jnp.where(mine[:, :, None], coded[None], 0), axis=1)
        coded = coded.reshape(1, tokens // LANES, LANES)
        coded = swap(jnp.broadcast_to(coded, (NX * NZ, *coded.shape[1:])), CORPUS)
        coded = jnp.sum(coded, axis=0).reshape(tokens)
        token_ids = coded // 2
        token_valid = coded % 2
        lengths = jnp.sum(token_valid.reshape(seq_count, seq_width), axis=1).astype(F32)
        survivor = x_index * n_mp + mp_index
        weight = lax.dynamic_index_in_dim(
            token_valid.reshape(seq_count, seq_width), survivor, 0, keepdims=False
        ).astype(F32) / lax.dynamic_index_in_dim(lengths, survivor, 0, keepdims=False)
        weight = jnp.broadcast_to(weight[:, None], (own_tokens, LANES))

    with jax.named_scope("passage_scores"):
        dots = lax.dot_general(
            question_word_vectors.reshape(-1, vector_dim),
            document_word_vectors.reshape(-1, vector_dim),
            TRANSPOSED,
            preferred_element_type=F32,
        ).reshape(query_count, -1, pass_count, pass_slots)
        slots = jnp.arange(pass_slots, dtype=jnp.int32)[None, :] < document_extent[:, None]
        best = jnp.max(jnp.where(slots[None, None], dots, F32(-1e30)), axis=3)
        scores = jnp.sum(best, axis=1).reshape(-1)
        rider = split3(scores).reshape(1, -1)
        rider = jnp.pad(rider, ((0, 7), (0, width - rider.shape[1])))

    with jax.named_scope("embedded"):
        local_ids = token_ids - corpus_index * vocab_rows
        chosen_rows = (
            local_ids[:, None] == jnp.arange(vocab_rows, dtype=jnp.int32)[None, :]
        ).astype(BF16)
        looked = jnp.dot(chosen_rows, vocab_lookup_table, preferred_element_type=F32).astype(BF16)
        looked = looked.reshape(NX, tokens // NX, width)
        looked = jnp.concatenate([looked, jnp.broadcast_to(rider[None], (NX, 8, width))], axis=1)
        looked = swap(looked, "x")
        rider = looked[:, tokens // NX].reshape(share, LANES)
        looked = jnp.sum(looked[:, : tokens // NX].astype(F32), axis=0).astype(BF16)
        looked = looked.reshape(NZ, share, width)
        looked = jnp.concatenate(
            [looked, jnp.broadcast_to(rider[None], (NZ, *rider.shape))], axis=2
        )
        looked = swap(looked, "z")
        rider = looked[:, :, width:]
        own = jnp.sum(looked[:, :, :width].astype(F32), axis=0)
        rows = share_with(own.astype(BF16), "z", NZ).reshape(-1, width)

    with jax.named_scope("shortlist"):
        table = jnp.sum(rider.reshape(NZ, NX, -1, LANES).astype(F32), axis=2)
        table = table.reshape(NZ, NX, query_count, pass_count)
        table = jnp.transpose(table, (2, 1, 0, 3)).reshape(query_count, -1, LANES)
        at_high = (shortlist_documents // LANES)[:, :, None] == jnp.arange(
            table.shape[1], dtype=jnp.int32
        )
        lines = lax.dot_general(
            at_high.astype(F32), table, (((2,), (1,)), ((0,), (0,))), precision=lax.Precision.HIGHEST
        )
        at_low = (shortlist_documents % LANES)[:, :, None] == jnp.arange(LANES, dtype=jnp.int32)
        picked = jnp.sum(jnp.where(at_low, lines, F32(0.0)), axis=2)
        picked = split3(picked.reshape(-1, LANES)).reshape(-1, LANES)
        pick_rows = picked.shape[0]
        picked = jnp.pad(picked, ((0, 2 * own_tokens - pick_rows), (0, 0)))
        picked = jnp.concatenate([picked[:own_tokens], picked[own_tokens:]], axis=1)

    vmem = pl.BlockSpec(memory_space=pltpu.VMEM)
    params = pltpu.CompilerParams(vmem_limit_bytes=32 << 20)
    own_rows = tokens // NX

    with jax.named_scope("gate_up"):
        part = pl.pallas_call(
            functools.partial(gate_up_kernel, n_mp, units),
            out_shape=jax.ShapeDtypeStruct((n_mp, own_tokens, 2 * half + 2 * LANES), BF16),
            in_specs=[vmem] * 7,
            out_specs=vmem,
            scratch_shapes=[pltpu.VMEM((2 * half, width), BF16), pltpu.VMEM((half, width), BF16)],
            compiler_params=params,
            cost_estimate=pl.CostEstimate(
                flops=4 * own_rows * width * half, bytes_accessed=4 << 20, transcendentals=0
            ),
        )(rows, gain, readout, *weights)
        part = swap(part, "mp")

    with jax.named_scope("hidden"):
        hidden = pl.pallas_call(
            functools.partial(hidden_kernel, n_mp, n_mp * width, half),
            out_shape=jax.ShapeDtypeStruct((own_tokens, half + 2 * LANES), BF16),
            in_specs=[vmem] * 3,
            out_specs=vmem,
            compiler_params=params,
            cost_estimate=pl.CostEstimate(
                flops=own_rows * half * 4, bytes_accessed=2 << 20, transcendentals=own_tokens * half
            ),
        )(part, weight, picked)
        hidden = share_with(hidden, "mp", n_mp)

    with jax.named_scope("down"):
        sent = pl.pallas_call(
            functools.partial(down_kernel, n_mp, units, half),
            out_shape=jax.ShapeDtypeStruct((NZ, share, width + LANES), BF16),
            in_specs=[vmem] * 5,
            out_specs=vmem,
            scratch_shapes=[pltpu.VMEM((half, width), BF16)],
            compiler_params=params,
            cost_estimate=pl.CostEstimate(
                flops=2 * own_rows * width * half, bytes_accessed=4 << 20, transcendentals=0
            ),
        )(hidden, *weights)
        got = swap(sent, "z")
        total = own + jnp.sum(got[:, :, :width].astype(F32), axis=0)
        layer_result = total.astype(BF16)

    with jax.named_scope("results"):
        picked = hidden[:, :, half:].reshape(n_mp, own_tokens, 2, LANES)
        picked = jnp.concatenate([picked[:, :, 0], picked[:, :, 1]], axis=1)[:, :pick_rows]
        picked = jnp.sum(picked.astype(F32).reshape(n_mp, 3, -1, LANES), axis=1)
        shortlist_maxsim = picked.reshape(n_mp * query_count, -1)
        merit = jnp.sum(got[:, :n_mp, width : width + 3].astype(F32), axis=(0, 2))
        merit = jnp.broadcast_to(jnp.pad(merit, (0, LANES - n_mp))[None], (8, LANES))
        merit = share_with(merit, "x", NX)[:, 0, :n_mp]

    return (shortlist_maxsim, layer_result, merit.reshape(retained_documents.shape))


def solution(mesh):
    split = Mesh(mesh.devices.reshape(NX, NZ, -1), ("x", "z", "mp"))
    placed = (
        P("mp", None, None),
        P(CORPUS, None, None),
        P(CORPUS),
        P("mp", None),
        P(),
        P(CORPUS, None),
        P(CORPUS, "mp"),
        P("mp"),
        P("mp", CORPUS),
        P("mp", CORPUS),
        P(CORPUS, "mp"),
        P("mp"),
    )
    return jax.shard_map(
        body, mesh=split, in_specs=placed, out_specs=(P(), P(CORPUS, "mp"), P()), check_vma=False
    )
```

```python
import functools

import jax
import jax.numpy as jnp
from jax import lax
from jax.experimental import pallas as pl
from jax.experimental.pallas import tpu as pltpu
from jax.sharding import Mesh, PartitionSpec as P

NX, NZ = 4, 16
LANES = 128
F32, BF16 = jnp.float32, jnp.bfloat16
CORPUS = ("x", "z")
TRANSPOSED = (((1,), (1,)), ((), ()))


def split3(v):
    high = lax.reduce_precision(v, 8, 7)
    rest = v - high
    mid = lax.reduce_precision(rest, 8, 7)
    low = lax.reduce_precision(rest - mid, 8, 7)
    return jnp.stack([high, mid, low]).astype(BF16)


def swap(v, axis):
    return lax.all_to_all(v, axis, 0, 0, tiled=True)


def share_with(v, axis, n):
    return swap(jnp.broadcast_to(v[None], (n, *v.shape)), axis)


def terms(v):
    high = v.astype(BF16).astype(F32)
    mid = (v - high).astype(BF16).astype(F32)
    return high, mid, v - high - mid


def fill(shape, axis, pieces):
    place = lax.broadcasted_iota(jnp.int32, shape, axis)
    block = jnp.zeros(shape, F32)
    for i, piece in enumerate(pieces):
        block = jnp.where(place == i, piece, block)
    return block


def ids_kernel(base_ref, chosen_ref, extent_ref, codes_ref, out_ref, wide, tile):
    slots, passes = codes_ref.shape
    each = LANES // slots
    wide[...] = jnp.concatenate([codes_ref[...]] * each, axis=0).T
    lane = lax.broadcasted_iota(jnp.int32, (1, LANES), 1)
    for row in range(tile.shape[0]):
        line = jnp.zeros((1, LANES), jnp.int32)
        for part in range(each):
            survivor = row * each + part
            kept = chosen_ref.shape[0]
            index = chosen_ref[survivor % kept, survivor // kept] - base_ref[0]
            held = (index >= 0) & (index < passes)
            index = jnp.clip(index, 0, passes - 1)
            first = part * slots
            here = (lane >= first) & (lane < jnp.where(held, first + slots, first))
            valid = (lane < first + extent_ref[index]).astype(jnp.int32)
            line = jnp.where(here, wide[pl.ds(index, 1), :] * 2 + valid, line)
        tile[row : row + 1, :] = line
    out_ref[...] = jnp.broadcast_to(tile[...][None], out_ref.shape)


def own_kernel(got_ref, own_ref, rows_ref, table_ref):
    width = own_ref.shape[1]
    total = got_ref[0, :, :width].astype(F32)
    for source in range(1, got_ref.shape[0]):
        total += got_ref[source, :, :width].astype(F32)
    own_ref[...] = total
    rows_ref[...] = jnp.broadcast_to(total.astype(BF16)[None], rows_ref.shape)
    scores = got_ref[:, :, width:].astype(F32)
    each = scores.shape[1] // NX
    queries = table_ref.shape[0]
    passes = LANES // queries
    lines = scores.shape[0] // queries
    for i in range(NX):
        value = jnp.sum(scores[:, i * each : (i + 1) * each], axis=1)
        value = value.reshape(lines, queries, LANES)
        for query in range(queries):
            take = slice(query * passes, (query + 1) * passes)
            table_ref[query, i * lines : (i + 1) * lines, :] = jnp.concatenate(
                [value[:, j, take] for j in range(queries)], axis=1
            )


def gather_rows(parts, start, stop, into, at):
    *whole, low, high = parts
    for part in whole:
        into[at : at + stop - start, :] = part[start:stop, :]
        at += stop - start
    middle = low.shape[0]
    if start < middle:
        end = min(stop, middle)
        into[at : at + end - start, :] = low[start:end, :]
        at += end - start
    if stop > middle:
        begin = max(start, middle)
        into[at : at + stop - begin, :] = high[begin - middle : stop - middle, :]


def gate_up_kernel(
    n_mp, units, rows_ref, gain_ref, readout_ref, w0_ref, w1_ref, w2_ref, w3_ref, w4_ref, out_ref,
    first, second,
):
    parts = (w0_ref, w1_ref, w2_ref, w3_ref, w4_ref)
    half = NX * units
    gather_rows(parts, 0, units, first, 0)
    gather_rows(parts, units, 2 * units, first, half)
    gather_rows(parts, 2 * units, 3 * units, second, 0)
    value = rows_ref[...].astype(F32)
    squares = jnp.sum(value * value, axis=1, keepdims=True)
    reading = jnp.sum(value * readout_ref[...], axis=1, keepdims=True)
    scaled = (value * gain_ref[...]).astype(BF16)
    both = lax.dot_general(scaled, first[...], TRANSPOSED, preferred_element_type=F32)
    per_token = fill((value.shape[0], LANES), 1, (*terms(squares), *terms(reading)))

    readout = fill((16, value.shape[1]), 0, terms(readout_ref[...])).astype(BF16)
    line = lax.dot_general(readout, second[...], TRANSPOSED, preferred_element_type=F32)
    line = jnp.sum(line, axis=0, keepdims=True)
    pieces = [
        term[:, at : at + LANES] for term in terms(line) for at in range(0, half, LANES)
    ]
    share = value.shape[0] // n_mp
    line = fill((share, LANES), 0, pieces).astype(BF16)
    for target in range(n_mp):
        take = slice(target * share, (target + 1) * share)
        out_ref[target, :, : 2 * half] = both[take].astype(BF16)
        out_ref[target, :, 2 * half : 2 * half + LANES] = per_token[take].astype(BF16)
        out_ref[target, :, 2 * half + LANES :] = line


def hidden_kernel(n_mp, features, half, got_ref, weight_ref, picks_ref, out_ref):
    total = got_ref[0].astype(F32)
    for source in range(1, n_mp):
        total += got_ref[source].astype(F32)
    per_token = total[:, 2 * half : 2 * half + LANES]
    lane = lax.broadcasted_iota(jnp.int32, per_token.shape, 1)
    squares = jnp.sum(jnp.where(lane < 3, per_token, 0.0), axis=1, keepdims=True)
    reading = jnp.sum(jnp.where((lane >= 3) & (lane < 6), per_token, 0.0), axis=1, keepdims=True)
    rscale = lax.rsqrt(squares / features + 1e-06)
    gate, up = rscale * total[:, :half], rscale * total[:, half : 2 * half]
    hidden = (gate / (1.0 + jnp.exp(-gate)) * up).astype(BF16)
    line = total[:, 2 * half + LANES :]
    count = half // LANES
    merit = reading * (1.0 / NZ)
    for i in range(count):
        piece = line[i : i + 1] + line[count + i : count + i + 1] + line[2 * count + i : 2 * count + i + 1]
        merit += jnp.sum(
            hidden[:, i * LANES : (i + 1) * LANES].astype(F32) * piece, axis=1, keepdims=True
        )
    merit = jnp.sum(merit * weight_ref[:, :1], axis=0, keepdims=True)
    place = lax.broadcasted_iota(jnp.int32, per_token.shape, 0)
    rider = picks_ref[:, LANES:].astype(F32)
    for i, term in enumerate(terms(merit)):
        rider = jnp.where(place == 16 + i, term, rider)
    out_ref[:, :half] = hidden
    out_ref[:, half : half + LANES] = picks_ref[:, :LANES]
    out_ref[:, half + LANES :] = rider.astype(BF16)


def down_kernel(
    n_mp, units, half, got_ref, w0_ref, w1_ref, w2_ref, w3_ref, w4_ref, out_ref, picks_ref, second
):
    parts = (w0_ref, w1_ref, w2_ref, w3_ref, w4_ref)
    gather_rows(parts, 2 * units, 3 * units, second, 0)
    tokens = got_ref.shape[0] * got_ref.shape[1]
    hidden = got_ref[:, :, :half].reshape(tokens, half)
    down = jnp.dot(hidden, second[...], preferred_element_type=F32)
    groups = out_ref.shape[0]
    share = tokens // groups
    shares = got_ref[:, 16:, half + LANES :].astype(F32)
    whole = got_ref[:, :, half : half + LANES].astype(F32)
    last = got_ref[:, :16, half + LANES :].astype(F32)
    picks = whole[:, :16] + whole[:, 16:] + last
    lines = picks_ref.shape[1] // LANES
    for i in range(picks_ref.shape[0]):
        at = i * lines % picks.shape[1]
        picks_ref[i : i + 1, :] = jnp.concatenate(
            [picks[i * lines // picks.shape[1], at + j : at + j + 1] for j in range(lines)], axis=1
        )
    rider = fill((n_mp, LANES), 1, (shares[:, 0], shares[:, 1], shares[:, 2]))
    rider = jnp.concatenate([rider, jnp.zeros((share - n_mp, LANES), F32)], axis=0).astype(BF16)
    for target in range(groups):
        out_ref[target, :, : down.shape[1]] = down[target * share : (target + 1) * share].astype(BF16)
        out_ref[target, :, down.shape[1] :] = rider


def body(
    question_word_vectors,
    document_word_vectors,
    document_extent,
    shortlist_documents,
    retained_documents,
    document_vocab_codes,
    vocab_lookup_table,
    prelayer_rms_gain,
    gating_projector,
    widening_projector,
    reducing_projector,
    merit_readout,
):
    n_mp = lax.axis_size("mp")
    x_index, z_index, mp_index = (lax.axis_index(name) for name in ("x", "z", "mp"))
    corpus_index = x_index * NZ + z_index
    query_count = question_word_vectors.shape[0]
    pass_count, pass_slots, vector_dim = document_word_vectors.shape
    vocab_rows, width = vocab_lookup_table.shape
    units = gating_projector.shape[1]
    half = NX * units
    seq_count = retained_documents.size
    seq_width = document_vocab_codes.shape[1]
    tokens = seq_count * seq_width
    share = tokens // (NX * NZ)
    own_tokens = tokens // NX // n_mp
    vmem = pl.BlockSpec(memory_space=pltpu.VMEM)
    smem = pl.BlockSpec(memory_space=pltpu.SMEM)

    with jax.named_scope("weights"):
        weights = [jnp.concatenate([gating_projector.T, widening_projector.T, reducing_projector], axis=0)]
        up = [(i, (i + 1) % NX) for i in range(NX)]
        down = [(i, (i - 1) % NX) for i in range(NX)]
        weights += [lax.ppermute(weights[0], "x", up), lax.ppermute(weights[0], "x", down)]
        gain = prelayer_rms_gain.astype(F32)[None]
        readout = merit_readout[None]

    with jax.named_scope("token_ids"):
        base = (corpus_index * pass_count).astype(jnp.int32).reshape(1)
        coded = pl.pallas_call(
            ids_kernel,
            out_shape=jax.ShapeDtypeStruct((NX * NZ, tokens // LANES, LANES), jnp.int32),
            in_specs=[smem] * 3 + [vmem],
            out_specs=vmem,
            scratch_shapes=[
                pltpu.VMEM((pass_count, LANES), jnp.int32),
                pltpu.VMEM((tokens // LANES, LANES), jnp.int32),
            ],
        )(base, retained_documents.T, document_extent, document_vocab_codes.T)
        coded = swap(coded, CORPUS)
        coded = jnp.sum(coded, axis=0).reshape(tokens)
        token_ids = coded // 2

    with jax.named_scope("passage_scores"):
        dots = lax.dot_general(
            question_word_vectors.reshape(-1, vector_dim),
            document_word_vectors.reshape(-1, vector_dim),
            TRANSPOSED,
            preferred_element_type=F32,
        ).reshape(query_count, -1, pass_count, pass_slots)
        slots = jnp.arange(pass_slots, dtype=jnp.int32)[None, :] < document_extent[:, None]
        best = jnp.max(jnp.where(slots[None, None], dots, F32(-1e30)), axis=3)
        scores = jnp.sum(best, axis=1).reshape(-1)
        rider = split3(scores).reshape(1, -1)
        rider = jnp.pad(rider, ((0, 7), (0, width - rider.shape[1])))

    with jax.named_scope("embedded"):
        local_ids = token_ids - corpus_index * vocab_rows
        chosen_rows = (
            local_ids[:, None] == jnp.arange(vocab_rows, dtype=jnp.int32)[None, :]
        ).astype(BF16)
        looked = jnp.dot(chosen_rows, vocab_lookup_table, preferred_element_type=F32).astype(BF16)
        looked = looked.reshape(NX, tokens // NX, width)
        looked = jnp.concatenate([looked, jnp.broadcast_to(rider[None], (NX, 8, width))], axis=1)
        looked = swap(looked, "x")
        rider = looked[:, tokens // NX].reshape(share, LANES)
        looked = jnp.sum(looked[:, : tokens // NX].astype(F32), axis=0).astype(BF16)
        looked = looked.reshape(NZ, share, width)
        looked = jnp.concatenate(
            [looked, jnp.broadcast_to(rider[None], (NZ, *rider.shape))], axis=2
        )
        looked = swap(looked, "z")
        own, rows, table = pl.pallas_call(
            own_kernel,
            out_shape=(
                jax.ShapeDtypeStruct((share, width), F32),
                jax.ShapeDtypeStruct((NZ, share, width), BF16),
                jax.ShapeDtypeStruct((query_count, NX * NZ * pass_count // LANES, LANES), F32),
            ),
            in_specs=[vmem],
            out_specs=(vmem, vmem, vmem),
        )(looked)
        rows, *weights = lax.optimization_barrier((rows, *weights))
        middle = weights[0].shape[0] // 2
        weights.append(lax.ppermute(weights[1][:middle], "x", up))
        weights.append(lax.ppermute(weights[2][middle:], "x", down))
        rows = swap(rows, "z").reshape(-1, width)

    params = pltpu.CompilerParams(vmem_limit_bytes=32 << 20)
    own_rows = tokens // NX

    with jax.named_scope("gate_up"):
        part = pl.pallas_call(
            functools.partial(gate_up_kernel, n_mp, units),
            out_shape=jax.ShapeDtypeStruct((n_mp, own_tokens, 2 * half + 2 * LANES), BF16),
            in_specs=[vmem] * 8,
            out_specs=vmem,
            scratch_shapes=[pltpu.VMEM((2 * half, width), BF16), pltpu.VMEM((half, width), BF16)],
            compiler_params=params,
            cost_estimate=pl.CostEstimate(
                flops=4 * own_rows * width * half, bytes_accessed=4 << 20, transcendentals=0
            ),
        )(rows, gain, readout, *weights)
        part, coded, table = lax.optimization_barrier((part, coded, table))
        part = swap(part, "mp")

    with jax.named_scope("token_weights"):
        token_valid = coded % 2
        lengths = jnp.sum(token_valid.reshape(seq_count, seq_width), axis=1).astype(F32)
        survivor = x_index * n_mp + mp_index
        weight = lax.dynamic_index_in_dim(
            token_valid.reshape(seq_count, seq_width), survivor, 0, keepdims=False
        ).astype(F32) / lax.dynamic_index_in_dim(lengths, survivor, 0, keepdims=False)
        weight = jnp.broadcast_to(weight[:, None], (own_tokens, LANES))

    with jax.named_scope("shortlist"):
        at_high = (shortlist_documents // LANES)[:, :, None] == jnp.arange(
            table.shape[1], dtype=jnp.int32
        )
        lines = lax.dot_general(
            at_high.astype(F32), table, (((2,), (1,)), ((0,), (0,))), precision=lax.Precision.HIGHEST
        )
        at_low = (shortlist_documents % LANES)[:, :, None] == jnp.arange(LANES, dtype=jnp.int32)
        picked = jnp.sum(jnp.where(at_low, lines, F32(0.0)), axis=2)
        picked = split3(picked.reshape(-1, LANES)).reshape(-1, LANES)
        picked = jnp.pad(picked, ((0, 2 * own_tokens - picked.shape[0]), (0, 0)))
        picked = jnp.concatenate([picked[:own_tokens], picked[own_tokens:]], axis=1)

    with jax.named_scope("hidden"):
        hidden = pl.pallas_call(
            functools.partial(hidden_kernel, n_mp, n_mp * width, half),
            out_shape=jax.ShapeDtypeStruct((own_tokens, half + 2 * LANES), BF16),
            in_specs=[vmem] * 3,
            out_specs=vmem,
            compiler_params=params,
            cost_estimate=pl.CostEstimate(
                flops=own_rows * half * 4, bytes_accessed=2 << 20, transcendentals=own_tokens * half
            ),
        )(part, weight, picked)
        hidden = share_with(hidden, "mp", n_mp)

    with jax.named_scope("down"):
        sent, shortlist_maxsim = pl.pallas_call(
            functools.partial(down_kernel, n_mp, units, half),
            out_shape=(
                jax.ShapeDtypeStruct((NZ, share, width + LANES), BF16),
                jax.ShapeDtypeStruct((n_mp * query_count, shortlist_documents.shape[1]), F32),
            ),
            in_specs=[vmem] * 6,
            out_specs=(vmem, vmem),
            scratch_shapes=[pltpu.VMEM((half, width), BF16)],
            compiler_params=params,
            cost_estimate=pl.CostEstimate(
                flops=2 * own_rows * width * half, bytes_accessed=4 << 20, transcendentals=0
            ),
        )(hidden, *weights)
        got = swap(sent, "z")
        total = own + jnp.sum(got[:, :, :width].astype(F32), axis=0)
        layer_result = total.astype(BF16)

    with jax.named_scope("results"):
        merit = jnp.sum(got[:, :n_mp, width : width + 3].astype(F32), axis=(0, 2))
        merit = jnp.broadcast_to(jnp.pad(merit, (0, LANES - n_mp))[None], (8, LANES))
        merit = share_with(merit, "x", NX)[:, 0, :n_mp]

    return (shortlist_maxsim, layer_result, merit.reshape(retained_documents.shape))


def solution(mesh):
    split = Mesh(mesh.devices.reshape(NX, NZ, -1), ("x", "z", "mp"))
    placed = (
        P("mp", None, None),
        P(CORPUS, None, None),
        P(CORPUS),
        P("mp", None),
        P(),
        P(CORPUS, None),
        P(CORPUS, "mp"),
        P("mp"),
        P("mp", CORPUS),
        P("mp", CORPUS),
        P(CORPUS, "mp"),
        P("mp"),
    )
    return jax.shard_map(
        body, mesh=split, in_specs=placed, out_specs=(P(), P(CORPUS, "mp"), P()), check_vma=False
    )
```

```python
import functools

import jax
import jax.numpy as jnp
from jax import lax
from jax.experimental import pallas as pl
from jax.experimental.pallas import tpu as pltpu
from jax.sharding import Mesh, PartitionSpec as P

NX, NZ = 4, 16
LANES = 128
F32, BF16 = jnp.float32, jnp.bfloat16
CORPUS = ("x", "z")
TRANSPOSED = (((1,), (1,)), ((), ()))


def split3(v):
    high = lax.reduce_precision(v, 8, 7)
    rest = v - high
    mid = lax.reduce_precision(rest, 8, 7)
    low = lax.reduce_precision(rest - mid, 8, 7)
    return jnp.stack([high, mid, low]).astype(BF16)


def swap(v, axis):
    return lax.all_to_all(v, axis, 0, 0, tiled=True)


def share_with(v, axis, n):
    return swap(jnp.broadcast_to(v[None], (n, *v.shape)), axis)


def terms(v):
    high = v.astype(BF16).astype(F32)
    mid = (v - high).astype(BF16).astype(F32)
    return high, mid, v - high - mid


def fill(shape, axis, pieces):
    place = lax.broadcasted_iota(jnp.int32, shape, axis)
    block = jnp.zeros(shape, F32)
    for i, piece in enumerate(pieces):
        block = jnp.where(place == i, piece, block)
    return block


def ids_kernel(base_ref, chosen_ref, extent_ref, codes_ref, out_ref, wide, tile):
    slots, passes = codes_ref.shape
    each = LANES // slots
    wide[...] = jnp.concatenate([codes_ref[...]] * each, axis=0).T
    lane = lax.broadcasted_iota(jnp.int32, (1, LANES), 1)
    for row in range(tile.shape[0]):
        line = jnp.zeros((1, LANES), jnp.int32)
        for part in range(each):
            survivor = row * each + part
            kept = chosen_ref.shape[0]
            index = chosen_ref[survivor % kept, survivor // kept] - base_ref[0]
            held = (index >= 0) & (index < passes)
            index = jnp.clip(index, 0, passes - 1)
            first = part * slots
            here = (lane >= first) & (lane < jnp.where(held, first + slots, first))
            valid = (lane < first + extent_ref[index]).astype(jnp.int32)
            line = jnp.where(here, wide[pl.ds(index, 1), :] * 2 + valid, line)
        tile[row : row + 1, :] = line
    out_ref[...] = jnp.broadcast_to(tile[...][None], out_ref.shape)


def own_kernel(got_ref, own_ref, rows_ref, table_ref):
    width = own_ref.shape[1]
    total = got_ref[0, :, :width].astype(F32)
    for source in range(1, got_ref.shape[0]):
        total += got_ref[source, :, :width].astype(F32)
    own_ref[...] = total
    rows_ref[...] = jnp.broadcast_to(total.astype(BF16)[None], rows_ref.shape)
    scores = got_ref[:, :, width:].astype(F32)
    each = scores.shape[1] // NX
    queries = table_ref.shape[0]
    passes = LANES // queries
    lines = scores.shape[0] // queries
    for i in range(NX):
        value = jnp.sum(scores[:, i * each : (i + 1) * each], axis=1)
        value = value.reshape(lines, queries, LANES)
        for query in range(queries):
            take = slice(query * passes, (query + 1) * passes)
            table_ref[query, i * lines : (i + 1) * lines, :] = jnp.concatenate(
                [value[:, j, take] for j in range(queries)], axis=1
            )


def gather_rows(parts, start, stop, into, at):
    *whole, low, high = parts
    for part in whole:
        into[at : at + stop - start, :] = part[start:stop, :]
        at += stop - start
    middle = low.shape[0]
    if start < middle:
        end = min(stop, middle)
        into[at : at + end - start, :] = low[start:end, :]
        at += end - start
    if stop > middle:
        begin = max(start, middle)
        into[at : at + stop - begin, :] = high[begin - middle : stop - middle, :]


def gate_up_kernel(
    n_mp, units, rows_ref, gain_ref, readout_ref, w0_ref, w1_ref, w2_ref, w3_ref, w4_ref, out_ref,
    first, second,
):
    parts = (w0_ref, w1_ref, w2_ref, w3_ref, w4_ref)
    half = NX * units
    gather_rows(parts, 0, units, first, 0)
    gather_rows(parts, units, 2 * units, first, half)
    gather_rows(parts, 2 * units, 3 * units, second, 0)
    value = rows_ref[...].astype(F32)
    squares = jnp.sum(value * value, axis=1, keepdims=True)
    reading = jnp.sum(value * readout_ref[...], axis=1, keepdims=True)
    scaled = (value * gain_ref[...]).astype(BF16)
    both = lax.dot_general(scaled, first[...], TRANSPOSED, preferred_element_type=F32)
    per_token = fill((value.shape[0], LANES), 1, (*terms(squares), *terms(reading)))

    readout = fill((16, value.shape[1]), 0, terms(readout_ref[...])).astype(BF16)
    line = lax.dot_general(readout, second[...], TRANSPOSED, preferred_element_type=F32)
    line = jnp.sum(line, axis=0, keepdims=True)
    pieces = [
        term[:, at : at + LANES] for term in terms(line) for at in range(0, half, LANES)
    ]
    share = value.shape[0] // n_mp
    line = fill((share, LANES), 0, pieces).astype(BF16)
    for target in range(n_mp):
        take = slice(target * share, (target + 1) * share)
        out_ref[target, :, : 2 * half] = both[take].astype(BF16)
        out_ref[target, :, 2 * half : 2 * half + LANES] = per_token[take].astype(BF16)
        out_ref[target, :, 2 * half + LANES :] = line


def hidden_kernel(n_mp, features, half, got_ref, weight_ref, picks_ref, out_ref):
    total = got_ref[0].astype(F32)
    for source in range(1, n_mp):
        total += got_ref[source].astype(F32)
    per_token = total[:, 2 * half : 2 * half + LANES]
    lane = lax.broadcasted_iota(jnp.int32, per_token.shape, 1)
    squares = jnp.sum(jnp.where(lane < 3, per_token, 0.0), axis=1, keepdims=True)
    reading = jnp.sum(jnp.where((lane >= 3) & (lane < 6), per_token, 0.0), axis=1, keepdims=True)
    rscale = lax.rsqrt(squares / features + 1e-06)
    gate, up = rscale * total[:, :half], rscale * total[:, half : 2 * half]
    hidden = (gate / (1.0 + jnp.exp(-gate)) * up).astype(BF16)
    line = total[:, 2 * half + LANES :]
    count = half // LANES
    merit = reading * (1.0 / NZ)
    for i in range(count):
        piece = line[i : i + 1] + line[count + i : count + i + 1] + line[2 * count + i : 2 * count + i + 1]
        merit += jnp.sum(
            hidden[:, i * LANES : (i + 1) * LANES].astype(F32) * piece, axis=1, keepdims=True
        )
    merit = jnp.sum(merit * weight_ref[:, :1], axis=0, keepdims=True)
    place = lax.broadcasted_iota(jnp.int32, per_token.shape, 0)
    rider = picks_ref[:, LANES:].astype(F32)
    for i, term in enumerate(terms(merit)):
        rider = jnp.where(place == 16 + i, term, rider)
    out_ref[:, :half] = hidden
    out_ref[:, half : half + LANES] = picks_ref[:, :LANES]
    out_ref[:, half + LANES :] = rider.astype(BF16)


def down_kernel(
    n_mp, units, half, got_ref, w0_ref, w1_ref, w2_ref, w3_ref, w4_ref, out_ref, picks_ref, second
):
    parts = (w0_ref, w1_ref, w2_ref, w3_ref, w4_ref)
    gather_rows(parts, 2 * units, 3 * units, second, 0)
    tokens = got_ref.shape[0] * got_ref.shape[1]
    hidden = got_ref[:, :, :half].reshape(tokens, half)
    down = jnp.dot(hidden, second[...], preferred_element_type=F32)
    groups = out_ref.shape[0]
    share = tokens // groups
    shares = got_ref[:, 16:, half + LANES :].astype(F32)
    whole = got_ref[:, :, half : half + LANES].astype(F32)
    last = got_ref[:, :16, half + LANES :].astype(F32)
    picks = whole[:, :16] + whole[:, 16:] + last
    lines = picks_ref.shape[1] // LANES
    for i in range(picks_ref.shape[0]):
        at = i * lines % picks.shape[1]
        picks_ref[i : i + 1, :] = jnp.concatenate(
            [picks[i * lines // picks.shape[1], at + j : at + j + 1] for j in range(lines)], axis=1
        )
    rider = fill((n_mp, LANES), 1, (shares[:, 0], shares[:, 1], shares[:, 2]))
    rider = jnp.concatenate([rider, jnp.zeros((share - n_mp, LANES), F32)], axis=0).astype(BF16)
    for target in range(groups):
        out_ref[target, :, : down.shape[1]] = down[target * share : (target + 1) * share].astype(BF16)
        out_ref[target, :, down.shape[1] :] = rider


def body(
    question_word_vectors,
    document_word_vectors,
    document_extent,
    shortlist_documents,
    retained_documents,
    document_vocab_codes,
    vocab_lookup_table,
    prelayer_rms_gain,
    gating_projector,
    widening_projector,
    reducing_projector,
    merit_readout,
):
    n_mp = lax.axis_size("mp")
    x_index, z_index, mp_index = (lax.axis_index(name) for name in ("x", "z", "mp"))
    corpus_index = x_index * NZ + z_index
    query_count = question_word_vectors.shape[0]
    pass_count, pass_slots, vector_dim = document_word_vectors.shape
    vocab_rows, width = vocab_lookup_table.shape
    units = gating_projector.shape[1]
    half = NX * units
    seq_count = retained_documents.size
    seq_width = document_vocab_codes.shape[1]
    tokens = seq_count * seq_width
    share = tokens // (NX * NZ)
    own_tokens = tokens // NX // n_mp
    vmem = pl.BlockSpec(memory_space=pltpu.VMEM)
    smem = pl.BlockSpec(memory_space=pltpu.SMEM)

    with jax.named_scope("weights"):
        weights = [jnp.concatenate([gating_projector.T, widening_projector.T, reducing_projector], axis=0)]
        up = [(i, (i + 1) % NX) for i in range(NX)]
        down = [(i, (i - 1) % NX) for i in range(NX)]
        weights += [lax.ppermute(weights[0], "x", up), lax.ppermute(weights[0], "x", down)]
        gain = prelayer_rms_gain.astype(F32)[None]
        readout = merit_readout[None]

    with jax.named_scope("token_ids"):
        base = (corpus_index * pass_count).astype(jnp.int32).reshape(1)
        coded = pl.pallas_call(
            ids_kernel,
            out_shape=jax.ShapeDtypeStruct((NZ, tokens // LANES, LANES), jnp.int32),
            in_specs=[smem] * 3 + [vmem],
            out_specs=vmem,
            scratch_shapes=[
                pltpu.VMEM((pass_count, LANES), jnp.int32),
                pltpu.VMEM((tokens // LANES, LANES), jnp.int32),
            ],
        )(base, retained_documents.T, document_extent, document_vocab_codes.T)
        coded = jnp.sum(swap(coded, "z"), axis=0)
        coded = jnp.sum(share_with(coded, "x", NX), axis=0).reshape(tokens)
        token_ids = coded // 2

    with jax.named_scope("passage_scores"):
        dots = lax.dot_general(
            question_word_vectors.reshape(-1, vector_dim),
            document_word_vectors.reshape(-1, vector_dim),
            TRANSPOSED,
            preferred_element_type=F32,
        ).reshape(query_count, -1, pass_count, pass_slots)
        slots = jnp.arange(pass_slots, dtype=jnp.int32)[None, :] < document_extent[:, None]
        best = jnp.max(jnp.where(slots[None, None], dots, F32(-1e30)), axis=3)
        scores = jnp.sum(best, axis=1).reshape(-1)
        rider = split3(scores).reshape(1, -1)
        rider = jnp.pad(rider, ((0, 7), (0, width - rider.shape[1])))

    with jax.named_scope("embedded"):
        local_ids = token_ids - corpus_index * vocab_rows
        chosen_rows = (
            local_ids[:, None] == jnp.arange(vocab_rows, dtype=jnp.int32)[None, :]
        ).astype(BF16)
        looked = jnp.dot(chosen_rows, vocab_lookup_table, preferred_element_type=F32).astype(BF16)
        looked = looked.reshape(NX, tokens // NX, width)
        looked = jnp.concatenate([looked, jnp.broadcast_to(rider[None], (NX, 8, width))], axis=1)
        looked = swap(looked, "x")
        rider = looked[:, tokens // NX].reshape(share, LANES)
        looked = jnp.sum(looked[:, : tokens // NX].astype(F32), axis=0).astype(BF16)
        looked = looked.reshape(NZ, share, width)
        looked = jnp.concatenate(
            [looked, jnp.broadcast_to(rider[None], (NZ, *rider.shape))], axis=2
        )
        looked = swap(looked, "z")
        own, rows, table = pl.pallas_call(
            own_kernel,
            out_shape=(
                jax.ShapeDtypeStruct((share, width), F32),
                jax.ShapeDtypeStruct((NZ, share, width), BF16),
                jax.ShapeDtypeStruct((query_count, NX * NZ * pass_count // LANES, LANES), F32),
            ),
            in_specs=[vmem],
            out_specs=(vmem, vmem, vmem),
        )(looked)
        rows, *weights = lax.optimization_barrier((rows, *weights))
        middle = weights[0].shape[0] // 2
        weights.append(lax.ppermute(weights[1][:middle], "x", up))
        weights.append(lax.ppermute(weights[2][middle:], "x", down))
        rows = swap(rows, "z").reshape(-1, width)

    params = pltpu.CompilerParams(vmem_limit_bytes=32 << 20)
    own_rows = tokens // NX

    with jax.named_scope("gate_up"):
        part = pl.pallas_call(
            functools.partial(gate_up_kernel, n_mp, units),
            out_shape=jax.ShapeDtypeStruct((n_mp, own_tokens, 2 * half + 2 * LANES), BF16),
            in_specs=[vmem] * 8,
            out_specs=vmem,
            scratch_shapes=[pltpu.VMEM((2 * half, width), BF16), pltpu.VMEM((half, width), BF16)],
            compiler_params=params,
            cost_estimate=pl.CostEstimate(
                flops=4 * own_rows * width * half, bytes_accessed=4 << 20, transcendentals=0
            ),
        )(rows, gain, readout, *weights)
        part, coded, table = lax.optimization_barrier((part, coded, table))
        part = swap(part, "mp")

    with jax.named_scope("token_weights"):
        token_valid = coded % 2
        lengths = jnp.sum(token_valid.reshape(seq_count, seq_width), axis=1).astype(F32)
        survivor = x_index * n_mp + mp_index
        weight = lax.dynamic_index_in_dim(
            token_valid.reshape(seq_count, seq_width), survivor, 0, keepdims=False
        ).astype(F32) / lax.dynamic_index_in_dim(lengths, survivor, 0, keepdims=False)
        weight = jnp.broadcast_to(weight[:, None], (own_tokens, LANES))

    with jax.named_scope("shortlist"):
        at_high = (shortlist_documents // LANES)[:, :, None] == jnp.arange(
            table.shape[1], dtype=jnp.int32
        )
        lines = lax.dot_general(
            at_high.astype(F32), table, (((2,), (1,)), ((0,), (0,))), precision=lax.Precision.HIGHEST
        )
        at_low = (shortlist_documents % LANES)[:, :, None] == jnp.arange(LANES, dtype=jnp.int32)
        picked = jnp.sum(jnp.where(at_low, lines, F32(0.0)), axis=2)
        picked = split3(picked.reshape(-1, LANES)).reshape(-1, LANES)
        picked = jnp.pad(picked, ((0, 2 * own_tokens - picked.shape[0]), (0, 0)))
        picked = jnp.concatenate([picked[:own_tokens], picked[own_tokens:]], axis=1)

    with jax.named_scope("hidden"):
        hidden = pl.pallas_call(
            functools.partial(hidden_kernel, n_mp, n_mp * width, half),
            out_shape=jax.ShapeDtypeStruct((own_tokens, half + 2 * LANES), BF16),
            in_specs=[vmem] * 3,
            out_specs=vmem,
            compiler_params=params,
            cost_estimate=pl.CostEstimate(
                flops=own_rows * half * 4, bytes_accessed=2 << 20, transcendentals=own_tokens * half
            ),
        )(part, weight, picked)
        hidden = share_with(hidden, "mp", n_mp)

    with jax.named_scope("down"):
        sent, shortlist_maxsim = pl.pallas_call(
            functools.partial(down_kernel, n_mp, units, half),
            out_shape=(
                jax.ShapeDtypeStruct((NZ, share, width + LANES), BF16),
                jax.ShapeDtypeStruct((n_mp * query_count, shortlist_documents.shape[1]), F32),
            ),
            in_specs=[vmem] * 6,
            out_specs=(vmem, vmem),
            scratch_shapes=[pltpu.VMEM((half, width), BF16)],
            compiler_params=params,
            cost_estimate=pl.CostEstimate(
                flops=2 * own_rows * width * half, bytes_accessed=4 << 20, transcendentals=0
            ),
        )(hidden, *weights)
        got = swap(sent, "z")
        total = own + jnp.sum(got[:, :, :width].astype(F32), axis=0)
        layer_result = total.astype(BF16)

    with jax.named_scope("results"):
        merit = jnp.sum(got[:, :n_mp, width : width + 3].astype(F32), axis=(0, 2))
        merit = jnp.broadcast_to(jnp.pad(merit, (0, LANES - n_mp))[None], (8, LANES))
        merit = share_with(merit, "x", NX)[:, 0, :n_mp]

    return (shortlist_maxsim, layer_result, merit.reshape(retained_documents.shape))


def solution(mesh):
    split = Mesh(mesh.devices.reshape(NX, NZ, -1), ("x", "z", "mp"))
    placed = (
        P("mp", None, None),
        P(CORPUS, None, None),
        P(CORPUS),
        P("mp", None),
        P(),
        P(CORPUS, None),
        P(CORPUS, "mp"),
        P("mp"),
        P("mp", CORPUS),
        P("mp", CORPUS),
        P(CORPUS, "mp"),
        P("mp"),
    )
    return jax.shard_map(
        body, mesh=split, in_specs=placed, out_specs=(P(), P(CORPUS, "mp"), P()), check_vma=False
    )
```

```python
import functools

import jax
import jax.numpy as jnp
from jax import lax
from jax.experimental import pallas as pl
from jax.experimental.pallas import tpu as pltpu
from jax.sharding import Mesh, PartitionSpec as P

NX, NZ = 4, 16
LANES = 128
F32, BF16 = jnp.float32, jnp.bfloat16
CORPUS = ("x", "z")
TRANSPOSED = (((1,), (1,)), ((), ()))


def split3(v):
    high = lax.reduce_precision(v, 8, 7)
    rest = v - high
    mid = lax.reduce_precision(rest, 8, 7)
    low = lax.reduce_precision(rest - mid, 8, 7)
    return jnp.stack([high, mid, low]).astype(BF16)


def swap(v, axis):
    return lax.all_to_all(v, axis, 0, 0, tiled=True)


def share_with(v, axis, n):
    return swap(jnp.broadcast_to(v[None], (n, *v.shape)), axis)


def terms(v):
    high = v.astype(BF16).astype(F32)
    mid = (v - high).astype(BF16).astype(F32)
    return high, mid, v - high - mid


def fill(shape, axis, pieces):
    place = lax.broadcasted_iota(jnp.int32, shape, axis)
    block = jnp.zeros(shape, F32)
    for i, piece in enumerate(pieces):
        block = jnp.where(place == i, piece, block)
    return block


def ids_kernel(base_ref, chosen_ref, extent_ref, codes_ref, out_ref, wide, tile):
    slots, passes = codes_ref.shape
    each = LANES // slots
    wide[...] = jnp.concatenate([codes_ref[...]] * each, axis=0).T
    lane = lax.broadcasted_iota(jnp.int32, (1, LANES), 1)
    for row in range(tile.shape[0]):
        line = jnp.zeros((1, LANES), jnp.int32)
        for part in range(each):
            survivor = row * each + part
            kept = chosen_ref.shape[0]
            index = chosen_ref[survivor % kept, survivor // kept] - base_ref[0]
            held = (index >= 0) & (index < passes)
            index = jnp.clip(index, 0, passes - 1)
            first = part * slots
            here = (lane >= first) & (lane < jnp.where(held, first + slots, first))
            valid = (lane < first + extent_ref[index]).astype(jnp.int32)
            line = jnp.where(here, wide[pl.ds(index, 1), :] * 2 + valid, line)
        tile[row : row + 1, :] = line
    out_ref[...] = jnp.broadcast_to(tile[...][None], out_ref.shape)


def own_kernel(got_ref, own_ref, rows_ref, table_ref):
    width = own_ref.shape[1]
    total = got_ref[0, :, :width].astype(F32)
    for source in range(1, got_ref.shape[0]):
        total += got_ref[source, :, :width].astype(F32)
    own_ref[...] = total
    rows_ref[...] = jnp.broadcast_to(total.astype(BF16)[None], rows_ref.shape)
    scores = got_ref[:, :, width:].astype(F32)
    each = scores.shape[1] // NX
    queries = table_ref.shape[0]
    passes = LANES // queries
    lines = scores.shape[0] // queries
    for i in range(NX):
        value = jnp.sum(scores[:, i * each : (i + 1) * each], axis=1)
        value = value.reshape(lines, queries, LANES)
        for query in range(queries):
            take = slice(query * passes, (query + 1) * passes)
            table_ref[query, i * lines : (i + 1) * lines, :] = jnp.concatenate(
                [value[:, j, take] for j in range(queries)], axis=1
            )


def gather_rows(parts, start, stop, into, at):
    *whole, low, high = parts
    for part in whole:
        into[at : at + stop - start, :] = part[start:stop, :]
        at += stop - start
    middle = low.shape[0]
    if start < middle:
        end = min(stop, middle)
        into[at : at + end - start, :] = low[start:end, :]
        at += end - start
    if stop > middle:
        begin = max(start, middle)
        into[at : at + stop - begin, :] = high[begin - middle : stop - middle, :]


def gate_up_kernel(
    n_mp, units, rows_ref, gain_ref, readout_ref, w0_ref, w1_ref, w2_ref, w3_ref, w4_ref, out_ref,
    first, second,
):
    parts = (w0_ref, w1_ref, w2_ref, w3_ref, w4_ref)
    half = NX * units
    gather_rows(parts, 0, units, first, 0)
    gather_rows(parts, units, 2 * units, first, half)
    gather_rows(parts, 2 * units, 3 * units, second, 0)
    value = rows_ref[...].astype(F32)
    squares = jnp.sum(value * value, axis=1, keepdims=True)
    reading = jnp.sum(value * readout_ref[...], axis=1, keepdims=True)
    scaled = (value * gain_ref[...]).astype(BF16)
    both = lax.dot_general(scaled, first[...], TRANSPOSED, preferred_element_type=F32)
    per_token = fill((value.shape[0], LANES), 1, (*terms(squares), *terms(reading)))

    readout = fill((16, value.shape[1]), 0, terms(readout_ref[...])).astype(BF16)
    line = lax.dot_general(readout, second[...], TRANSPOSED, preferred_element_type=F32)
    line = jnp.sum(line, axis=0, keepdims=True)
    pieces = [
        term[:, at : at + LANES] for term in terms(line) for at in range(0, half, LANES)
    ]
    share = value.shape[0] // n_mp
    line = fill((share, LANES), 0, pieces).astype(BF16)
    for target in range(n_mp):
        take = slice(target * share, (target + 1) * share)
        out_ref[target, :, : 2 * half] = both[take].astype(BF16)
        out_ref[target, :, 2 * half : 2 * half + LANES] = per_token[take].astype(BF16)
        out_ref[target, :, 2 * half + LANES :] = line


def hidden_kernel(n_mp, features, half, got_ref, weight_ref, picks_ref, out_ref):
    total = got_ref[0].astype(F32)
    for source in range(1, n_mp):
        total += got_ref[source].astype(F32)
    per_token = total[:, 2 * half : 2 * half + LANES]
    lane = lax.broadcasted_iota(jnp.int32, per_token.shape, 1)
    squares = jnp.sum(jnp.where(lane < 3, per_token, 0.0), axis=1, keepdims=True)
    reading = jnp.sum(jnp.where((lane >= 3) & (lane < 6), per_token, 0.0), axis=1, keepdims=True)
    rscale = lax.rsqrt(squares / features + 1e-06)
    gate, up = rscale * total[:, :half], rscale * total[:, half : 2 * half]
    hidden = (gate / (1.0 + jnp.exp(-gate)) * up).astype(BF16)
    line = total[:, 2 * half + LANES :]
    count = half // LANES
    merit = reading * (1.0 / NZ)
    for i in range(count):
        piece = line[i : i + 1] + line[count + i : count + i + 1] + line[2 * count + i : 2 * count + i + 1]
        merit += jnp.sum(
            hidden[:, i * LANES : (i + 1) * LANES].astype(F32) * piece, axis=1, keepdims=True
        )
    merit = jnp.sum(merit * weight_ref[:, :1], axis=0, keepdims=True)
    place = lax.broadcasted_iota(jnp.int32, per_token.shape, 0)
    rider = picks_ref[:, LANES:].astype(F32)
    for i, term in enumerate(terms(merit)):
        rider = jnp.where(place == 16 + i, term, rider)
    out_ref[:, :half] = hidden
    out_ref[:, half : half + LANES] = picks_ref[:, :LANES]
    out_ref[:, half + LANES :] = rider.astype(BF16)


def down_kernel(
    n_mp, units, half, got_ref, w0_ref, w1_ref, w2_ref, w3_ref, w4_ref, out_ref, picks_ref, second
):
    parts = (w0_ref, w1_ref, w2_ref, w3_ref, w4_ref)
    gather_rows(parts, 2 * units, 3 * units, second, 0)
    tokens = got_ref.shape[0] * got_ref.shape[1]
    hidden = got_ref[:, :, :half].reshape(tokens, half)
    down = jnp.dot(hidden, second[...], preferred_element_type=F32)
    groups = out_ref.shape[0]
    share = tokens // groups
    shares = got_ref[:, 16:, half + LANES :].astype(F32)
    whole = got_ref[:, :, half : half + LANES].astype(F32)
    last = got_ref[:, :16, half + LANES :].astype(F32)
    picks = whole[:, :16] + whole[:, 16:] + last
    lines = picks_ref.shape[1] // LANES
    for i in range(picks_ref.shape[0]):
        at = i * lines % picks.shape[1]
        picks_ref[i : i + 1, :] = jnp.concatenate(
            [picks[i * lines // picks.shape[1], at + j : at + j + 1] for j in range(lines)], axis=1
        )
    rider = fill((n_mp, LANES), 1, (shares[:, 0], shares[:, 1], shares[:, 2]))
    rider = rider.astype(BF16)
    for target in range(groups):
        block = down[target * share : (target + 1) * share].astype(BF16)
        for part in range(down.shape[1] // LANES):
            rows = slice(part * share, (part + 1) * share)
            out_ref[target, rows, :] = block[:, part * LANES : (part + 1) * LANES]
        out_ref[target, out_ref.shape[1] - n_mp :, :] = rider


def body(
    question_word_vectors,
    document_word_vectors,
    document_extent,
    shortlist_documents,
    retained_documents,
    document_vocab_codes,
    vocab_lookup_table,
    prelayer_rms_gain,
    gating_projector,
    widening_projector,
    reducing_projector,
    merit_readout,
):
    n_mp = lax.axis_size("mp")
    x_index, z_index, mp_index = (lax.axis_index(name) for name in ("x", "z", "mp"))
    corpus_index = x_index * NZ + z_index
    query_count = question_word_vectors.shape[0]
    pass_count, pass_slots, vector_dim = document_word_vectors.shape
    vocab_rows, width = vocab_lookup_table.shape
    units = gating_projector.shape[1]
    half = NX * units
    seq_count = retained_documents.size
    seq_width = document_vocab_codes.shape[1]
    tokens = seq_count * seq_width
    share = tokens // (NX * NZ)
    own_tokens = tokens // NX // n_mp
    vmem = pl.BlockSpec(memory_space=pltpu.VMEM)
    smem = pl.BlockSpec(memory_space=pltpu.SMEM)

    with jax.named_scope("weights"):
        weights = [jnp.concatenate([gating_projector.T, widening_projector.T, reducing_projector], axis=0)]
        up = [(i, (i + 1) % NX) for i in range(NX)]
        down = [(i, (i - 1) % NX) for i in range(NX)]
        weights += [lax.ppermute(weights[0], "x", up), lax.ppermute(weights[0], "x", down)]
        gain = prelayer_rms_gain.astype(F32)[None]
        readout = merit_readout[None]

    with jax.named_scope("token_ids"):
        base = (corpus_index * pass_count).astype(jnp.int32).reshape(1)
        coded = pl.pallas_call(
            ids_kernel,
            out_shape=jax.ShapeDtypeStruct((NZ, tokens // LANES, LANES), jnp.int32),
            in_specs=[smem] * 3 + [vmem],
            out_specs=vmem,
            scratch_shapes=[
                pltpu.VMEM((pass_count, LANES), jnp.int32),
                pltpu.VMEM((tokens // LANES, LANES), jnp.int32),
            ],
        )(base, retained_documents.T, document_extent, document_vocab_codes.T)
        coded = jnp.sum(swap(coded, "z"), axis=0)
        coded = lax.psum(coded, "x").reshape(tokens)
        token_ids = coded // 2

    with jax.named_scope("passage_scores"):
        dots = lax.dot_general(
            question_word_vectors.reshape(-1, vector_dim),
            document_word_vectors.reshape(-1, vector_dim),
            TRANSPOSED,
            preferred_element_type=F32,
        ).reshape(query_count, -1, pass_count, pass_slots)
        slots = jnp.arange(pass_slots, dtype=jnp.int32)[None, :] < document_extent[:, None]
        best = jnp.max(jnp.where(slots[None, None], dots, F32(-1e30)), axis=3)
        scores = jnp.sum(best, axis=1).reshape(-1)
        rider = split3(scores).reshape(1, -1)
        rider = jnp.pad(rider, ((0, 7), (0, width - rider.shape[1])))

    with jax.named_scope("embedded"):
        local_ids = token_ids - corpus_index * vocab_rows
        chosen_rows = (
            local_ids[:, None] == jnp.arange(vocab_rows, dtype=jnp.int32)[None, :]
        ).astype(BF16)
        looked = jnp.dot(chosen_rows, vocab_lookup_table, preferred_element_type=F32).astype(BF16)
        looked = looked.reshape(NX, tokens // NX, width)
        looked = jnp.concatenate([looked, jnp.broadcast_to(rider[None], (NX, 8, width))], axis=1)
        looked = swap(looked, "x")
        rider = looked[:, tokens // NX].reshape(share, LANES)
        looked = jnp.sum(looked[:, : tokens // NX].astype(F32), axis=0).astype(BF16)
        looked = looked.reshape(NZ, share, width)
        looked = jnp.concatenate(
            [looked, jnp.broadcast_to(rider[None], (NZ, *rider.shape))], axis=2
        )
        looked = swap(looked, "z")
        own, rows, table = pl.pallas_call(
            own_kernel,
            out_shape=(
                jax.ShapeDtypeStruct((share, width), F32),
                jax.ShapeDtypeStruct((NZ, share, width), BF16),
                jax.ShapeDtypeStruct((query_count, NX * NZ * pass_count // LANES, LANES), F32),
            ),
            in_specs=[vmem],
            out_specs=(vmem, vmem, vmem),
        )(looked)
        rows, *weights = lax.optimization_barrier((rows, *weights))
        middle = weights[0].shape[0] // 2
        weights.append(lax.ppermute(weights[1][:middle], "x", up))
        weights.append(lax.ppermute(weights[2][middle:], "x", down))
        rows = swap(rows, "z").reshape(-1, width)

    params = pltpu.CompilerParams(vmem_limit_bytes=32 << 20)
    own_rows = tokens // NX

    with jax.named_scope("gate_up"):
        part = pl.pallas_call(
            functools.partial(gate_up_kernel, n_mp, units),
            out_shape=jax.ShapeDtypeStruct((n_mp, own_tokens, 2 * half + 2 * LANES), BF16),
            in_specs=[vmem] * 8,
            out_specs=vmem,
            scratch_shapes=[pltpu.VMEM((2 * half, width), BF16), pltpu.VMEM((half, width), BF16)],
            compiler_params=params,
            cost_estimate=pl.CostEstimate(
                flops=4 * own_rows * width * half, bytes_accessed=4 << 20, transcendentals=0
            ),
        )(rows, gain, readout, *weights)
        part, coded, table = lax.optimization_barrier((part, coded, table))
        part = swap(part, "mp")

    with jax.named_scope("token_weights"):
        token_valid = coded % 2
        lengths = jnp.sum(token_valid.reshape(seq_count, seq_width), axis=1).astype(F32)
        survivor = x_index * n_mp + mp_index
        weight = lax.dynamic_index_in_dim(
            token_valid.reshape(seq_count, seq_width), survivor, 0, keepdims=False
        ).astype(F32) / lax.dynamic_index_in_dim(lengths, survivor, 0, keepdims=False)
        weight = jnp.broadcast_to(weight[:, None], (own_tokens, LANES))

    with jax.named_scope("shortlist"):
        at_high = (shortlist_documents // LANES)[:, :, None] == jnp.arange(
            table.shape[1], dtype=jnp.int32
        )
        lines = lax.dot_general(
            at_high.astype(F32), table, (((2,), (1,)), ((0,), (0,))), precision=lax.Precision.HIGHEST
        )
        at_low = (shortlist_documents % LANES)[:, :, None] == jnp.arange(LANES, dtype=jnp.int32)
        picked = jnp.sum(jnp.where(at_low, lines, F32(0.0)), axis=2)
        picked = split3(picked.reshape(-1, LANES)).reshape(-1, LANES)
        picked = jnp.pad(picked, ((0, 2 * own_tokens - picked.shape[0]), (0, 0)))
        picked = jnp.concatenate([picked[:own_tokens], picked[own_tokens:]], axis=1)

    with jax.named_scope("hidden"):
        hidden = pl.pallas_call(
            functools.partial(hidden_kernel, n_mp, n_mp * width, half),
            out_shape=jax.ShapeDtypeStruct((own_tokens, half + 2 * LANES), BF16),
            in_specs=[vmem] * 3,
            out_specs=vmem,
            compiler_params=params,
            cost_estimate=pl.CostEstimate(
                flops=own_rows * half * 4, bytes_accessed=2 << 20, transcendentals=own_tokens * half
            ),
        )(part, weight, picked)
        hidden = share_with(hidden, "mp", n_mp)

    with jax.named_scope("down"):
        sent, shortlist_maxsim = pl.pallas_call(
            functools.partial(down_kernel, n_mp, units, half),
            out_shape=(
                jax.ShapeDtypeStruct((NZ, share * width // LANES + n_mp, LANES), BF16),
                jax.ShapeDtypeStruct((n_mp * query_count, shortlist_documents.shape[1]), F32),
            ),
            in_specs=[vmem] * 6,
            out_specs=(vmem, vmem),
            scratch_shapes=[pltpu.VMEM((half, width), BF16)],
            compiler_params=params,
            cost_estimate=pl.CostEstimate(
                flops=2 * own_rows * width * half, bytes_accessed=4 << 20, transcendentals=0
            ),
        )(hidden, *weights)
        got = swap(sent, "z")
        total = jnp.sum(got[:, :-n_mp].astype(F32), axis=0).reshape(-1, share, LANES)
        total = own + jnp.transpose(total, (1, 0, 2)).reshape(share, width)
        layer_result = total.astype(BF16)

    with jax.named_scope("results"):
        merit = jnp.sum(got[:, -n_mp:, :3].astype(F32), axis=(0, 2))
        merit = jnp.broadcast_to(jnp.pad(merit, (0, LANES - n_mp))[None], (8, LANES))
        merit = share_with(merit, "x", NX)[:, 0, :n_mp]

    return (shortlist_maxsim, layer_result, merit.reshape(retained_documents.shape))


def solution(mesh):
    split = Mesh(mesh.devices.reshape(NX, NZ, -1), ("x", "z", "mp"))
    placed = (
        P("mp", None, None),
        P(CORPUS, None, None),
        P(CORPUS),
        P("mp", None),
        P(),
        P(CORPUS, None),
        P(CORPUS, "mp"),
        P("mp"),
        P("mp", CORPUS),
        P("mp", CORPUS),
        P(CORPUS, "mp"),
        P("mp"),
    )
    return jax.shard_map(
        body, mesh=split, in_specs=placed, out_specs=(P(), P(CORPUS, "mp"), P()), check_vma=False
    )
```
